32 devices in a mesh: groups: 2 (over x), sec: 16 (over z, y, core).
Axes of the slice: x: 2, y: 2, z: 4, core: 2. Of those that a mesh axis runs over, the one named last changes fastest.
Arguments:
- two_site: bfloat16 [64, 256, 256], P(('groups', 'sec')), parts along dimension 0, may hold values from -6 to 6
- left_size: int32 [64], P(('groups', 'sec')), parts along dimension 0, may hold values from 64 to 256, as said below
- right_size: int32 [64], P(('groups', 'sec')), parts along dimension 0, may hold values from 64 to 256, as said below
- term_shift: int32 [48], P('groups'), parts along dimension 0, may hold values from -1 to 1
- route_offset: int32 [96], P('groups'), parts along dimension 0, may hold values from 0 to 15, as said below
- left_env: bfloat16 [64, 24, 256, 256], P(('groups', 'sec')), parts along dimension 0, may hold values from -0.375 to 0.375
- right_env: bfloat16 [1536, 256, 256], P(('groups', 'sec')), parts along dimension 0, may hold values from -0.078125 to 0.078125
Outputs:
- hamiltonian_theta: bfloat16 [64, 256, 256], P(('groups', 'sec')), parts along dimension 0
The draws below stay inside these ranges and needn't reach their ends.
There are 2 independent parts, one for each index of `groups`. The reference program is written for one: setup_inputs(seed, part) draws one part's arguments, and reference() takes and returns one part's arrays. A program takes and returns all parts, laid end to end along the dimension named above; each array names one. Nothing has to cross between parts.
Inputs may be any that keep to these rules, and one draw needn't show every extreme that they name: `left_size`: some sector has 256 live left states. `right_size`: some sector has 256 live right states. `route_offset`: each value appears at most 3 times and some value exactly 3 times.
All inputs are finite; a program needn't handle non-finite values.
Results may differ from the reference program's by a relative error of at most 0.01.
Values may be sent and summed in bfloat16 or wider, within the bound.
A program may use at most 128 MiB of HBM per device.

```python
import jax
import jax.numpy as jnp
from jax import lax

SEC_DEV = 2
STATES = 256
TERMS = 24
SECTORS = 32
UNITS = 48
SLOTS = 3
N_SEC = 16


def sector_sizes(key):
    first_key, second_key = jax.random.split(key)
    values_drawn = jax.random.randint(first_key, (SECTORS,), STATES // 4, STATES + 1)
    chosen_index = jax.random.randint(second_key, (), 0, SECTORS)
    return jnp.where(jnp.arange(SECTORS) == chosen_index, STATES, values_drawn).astype(jnp.int32)


def draw_left_size(key, part):
    key = jax.random.fold_in(key, 11)
    return sector_sizes(key)


def draw_right_size(key, part):
    key = jax.random.fold_in(key, 12)
    return sector_sizes(key)


def draw_route_offset(key, part):
    key = jax.random.fold_in(key, 13)
    first_key, second_key, third_key = jax.random.split(key, 3)
    slot_total = N_SEC * SLOTS
    full_value = jax.random.randint(first_key, (), 0, N_SEC)
    scores = jax.random.permutation(second_key, slot_total)
    scores = jnp.where(jnp.arange(slot_total) // SLOTS == full_value, scores - slot_total, scores)
    ordering = jnp.argsort(scores)
    chosen = ordering[:UNITS]
    chosen = chosen[jax.random.permutation(third_key, UNITS)]
    return (chosen // SLOTS).astype(jnp.int32)


def plant(entries, stream_key, least, high):
    extent = entries.shape
    place = [jax.random.randint(jax.random.fold_in(stream_key, axis), (), 0, extent[axis]) for axis in range(len(extent))]
    entries = entries.at[tuple(place)].set(least)
    longest = extent.index(max(extent))
    place[longest] = (place[longest] + 1) % extent[longest]
    return entries.at[tuple(place)].set(high)


def shard_levels(stream_key, shape, pieces, low, high):
    gain = 1.0
    for dim, shards_of in pieces:
        draws = jax.random.uniform(jax.random.fold_in(jax.random.fold_in(stream_key, 6), dim), (shards_of,), jnp.float32, low / len(pieces), high / len(pieces))
        gain = gain * jnp.repeat(jnp.exp(draws), shape[dim] // shards_of).reshape((-1,) + (1,) * (len(shape) - 1 - dim))
    return gain


def gaussian(key, shape, width, bound, cuts=(), kind=jnp.bfloat16):
    values = jax.random.normal(key, shape, jnp.float32) * width
    if len(cuts) > 0:
        values = shard_levels(key, shape, cuts, -0.22, 0.18) * values
    return jnp.clip(values, min=-bound, max=bound).astype(kind)


def setup_inputs(seed: int = 0, part: int = 0) -> dict:
    arg_keys = jax.random.split(jax.random.key(seed), 8)
    part_keys = jax.random.split(jax.random.fold_in(arg_keys[7], part), 8)
    two_site = gaussian(part_keys[0], (SECTORS, STATES, STATES), 1.0, 6.0, ((0, 16),))
    left_size = draw_left_size(jax.random.fold_in(jax.random.fold_in(arg_keys[7], part), 71), part)
    right_size = draw_right_size(jax.random.fold_in(jax.random.fold_in(arg_keys[7], part), 71), part)
    term_shift = plant(jax.random.randint(part_keys[3], (TERMS,), -1, 2), jax.random.fold_in(part_keys[3], 1), -1, 1).astype(jnp.int32)
    route_offset = draw_route_offset(jax.random.fold_in(jax.random.fold_in(arg_keys[7], part), 71), part)
    left_env = gaussian(part_keys[5], (SECTORS, TERMS, STATES, STATES), STATES ** -0.5, 0.375, ((0, 16),))
    right_env = gaussian(part_keys[6], (SECTORS * TERMS, STATES, STATES), (STATES * TERMS) ** -0.5, 0.078125, ((0, 16),))
    return {"two_site": two_site, "left_size": left_size, "right_size": right_size, "term_shift": term_shift, "route_offset": route_offset, "left_env": left_env, "right_env": right_env}


def live_region(left_size, right_size, states):
    positions = jnp.arange(states, dtype=jnp.int32)
    return (positions[None, :, None] < left_size[:, None, None]) & (positions[None, None, :] < right_size[:, None, None])


def reference(two_site, left_size, right_size, term_shift, route_offset, left_env, right_env):
    live_mask = live_region(left_size, right_size, STATES)
    masked = jnp.where(live_mask, two_site, jnp.zeros_like(two_site))
    border = jnp.zeros((1, STATES, STATES), two_site.dtype)
    padded = jnp.concatenate([border, masked, border], axis=0)
    unit_index = jnp.arange(SEC_DEV * TERMS, dtype=jnp.int32)
    local_sector = unit_index // TERMS
    shifts = jnp.tile(term_shift, SEC_DEV)

    def one_device(device):
        source_index = (device * SEC_DEV + local_sector + 1 - shifts).astype(jnp.int32)
        sources = jnp.take(padded, source_index, axis=0)
        left_blocks = lax.dynamic_slice_in_dim(left_env, (device * SEC_DEV).astype(jnp.int32), SEC_DEV, 0)
        left_blocks = left_blocks.reshape(SEC_DEV * TERMS, STATES, STATES)
        projected = jnp.einsum("uab,ubc->uac", left_blocks.astype(jnp.float32), sources.astype(jnp.float32)).astype(jnp.bfloat16)
        worker = jnp.mod(device + route_offset, N_SEC).astype(jnp.int32)
        right_blocks = jnp.take(right_env, (worker * (SEC_DEV * TERMS) + unit_index).astype(jnp.int32), axis=0)
        term_result = jnp.einsum("uab,ucb->uac", projected.astype(jnp.float32), right_blocks.astype(jnp.float32)).astype(jnp.bfloat16)
        return jnp.sum(term_result.astype(jnp.float32).reshape(SEC_DEV, TERMS, STATES, STATES), axis=1)

    summed = lax.map(one_device, jnp.arange(N_SEC, dtype=jnp.int32)).reshape(SECTORS, STATES, STATES)
    return jnp.where(live_mask, summed, jnp.zeros_like(summed)).astype(jnp.bfloat16)
```

```python
import functools

import jax
import jax.numpy as jnp
from jax import lax
from jax.experimental import pallas as pl
from jax.experimental.pallas import tpu as pltpu
from jax.sharding import PartitionSpec as P


def live_region(rows, columns, states):
    row = lax.broadcasted_iota(jnp.int32, (states, states), 0)
    column = lax.broadcasted_iota(jnp.int32, (states, states), 1)
    return (row < rows) & (column < columns)


def kernel(
    members,
    slots,
    picked_ref,
    shift_ref,
    left_size_ref,
    right_size_ref,
    two_site_ref,
    left_env_ref,
    right_env_ref,
    out_ref,
    left_vmem,
    right_vmem,
    outgoing,
    incoming,
    projected,
    padded,
    total,
    left_sem,
    right_sem,
    edge_send_sem,
    edge_recv_sem,
    send_sem,
    recv_sem,
):
    own = lax.axis_index("sec")
    sec_local, states = two_site_ref.shape[0], two_site_ref.shape[1]
    unit_count = left_env_ref.shape[0]
    term_count = unit_count // sec_local

    right_copy = pltpu.make_async_copy(right_env_ref, right_vmem, right_sem)
    right_copy.start()
    left_copy = pltpu.make_async_copy(left_env_ref, left_vmem, left_sem)
    left_copy.start()

    barrier = pltpu.get_barrier_semaphore()

    def greet(step, carry):
        peer = lax.rem(own + step, members)
        pl.semaphore_signal(barrier, inc=1, device_id={"sec": peer})
        return carry

    lax.fori_loop(1, members, greet, 0)

    for sector in range(sec_local):
        live = live_region(left_size_ref[sector], right_size_ref[sector], states)
        block = two_site_ref[sector]
        padded[1 + sector] = jnp.where(live, block, jnp.zeros_like(block))

    pl.semaphore_wait(barrier, members - 1)

    def edge_copy(source, target, index, peer):
        return pltpu.make_async_remote_copy(
            src_ref=padded.at[source],
            dst_ref=padded.at[target],
            send_sem=edge_send_sem.at[index],
            recv_sem=edge_recv_sem.at[index],
            device_id={"sec": peer},
        )

    up = edge_copy(sec_local, 0, 0, lax.rem(own + 1, members))
    down = edge_copy(1, sec_local + 1, 1, lax.rem(own + members - 1, members))
    has_up, has_down = own < members - 1, own > 0

    pl.when(has_up)(up.start)
    pl.when(has_down)(down.start)

    def block_copy(offset, peer):
        return pltpu.make_async_remote_copy(
            src_ref=outgoing.at[pl.ds(offset * slots, slots)],
            dst_ref=incoming.at[pl.ds(offset * slots, slots)],
            send_sem=send_sem.at[offset],
            recv_sem=recv_sem.at[offset],
            device_id={"sec": peer},
        )

    right_copy.wait()

    def order(step):
        return lax.rem(members // 2 + step, members)

    def send(step, carry):
        offset = order(step)

        @pl.when(offset > 0)
        def _():
            for slot in range(slots):
                unit = jnp.minimum(picked_ref[offset * slots + slot], unit_count - 1)
                outgoing[offset * slots + slot] = right_vmem[unit]
            block_copy(offset, lax.rem(own - offset + members, members)).start()

        @pl.when(offset == 0)
        def _():
            for slot in range(slots):
                unit = jnp.minimum(picked_ref[slot], unit_count - 1)
                incoming[slot] = right_vmem[unit]

        return carry

    lax.fori_loop(0, members, send, 0)

    @pl.when(own == 0)
    def _():
        padded[0] = jnp.zeros_like(padded[0])

    @pl.when(own == members - 1)
    def _():
        padded[sec_local + 1] = jnp.zeros_like(padded[0])

    pl.when(has_up)(up.wait_send)
    pl.when(has_down)(down.wait_send)
    pl.when(has_down)(up.wait_recv)
    pl.when(has_up)(down.wait_recv)
    left_copy.wait()

    def project(unit, carry):
        source = padded[unit // term_count + 1 - shift_ref[unit % term_count]]
        projected[unit] = jnp.dot(
            left_vmem[unit], source, preferred_element_type=jnp.float32
        ).astype(jnp.bfloat16)
        return carry

    lax.fori_loop(0, unit_count, project, 0)

    total[...] = jnp.zeros_like(total)

    def multiply(offset):
        for slot in range(slots):
            unit = picked_ref[offset * slots + slot]
            factor = projected[jnp.minimum(unit, unit_count - 1)]
            value = lax.dot_general(
                factor,
                incoming[offset * slots + slot],
                (((1,), (1,)), ((), ())),
                preferred_element_type=jnp.float32,
            )
            for sector in range(sec_local):
                mine = unit // term_count == sector
                total[sector] += jnp.where(mine, value, jnp.zeros_like(value))

    multiply(0)

    def arrive(step, carry):
        half = step // 2
        offset = jnp.where(step % 2 == 0, half + 1, members - 1 - half)
        block_copy(offset, lax.rem(own - offset + members, members)).wait_recv()
        multiply(offset)
        return carry

    lax.fori_loop(0, members - 1, arrive, 0)

    def sent(offset, carry):
        block_copy(offset, lax.rem(own - offset + members, members)).wait_send()
        return carry

    lax.fori_loop(1, members, sent, 0)

    for sector in range(sec_local):
        live = live_region(left_size_ref[sector], right_size_ref[sector], states)
        value = total[sector]
        out_ref[sector] = jnp.where(live, value, jnp.zeros_like(value)).astype(out_ref.dtype)


def local(two_site, left_size, right_size, term_shift, route_offset, left_env, right_env):
    members = lax.axis_size("sec")
    sec_local, states = two_site.shape[0], two_site.shape[1]
    unit_count = right_env.shape[0]
    slots = (unit_count + members - 1) // members
    slot_total = members * slots
    unit_index = jnp.arange(unit_count, dtype=jnp.int32)
    same_offset = route_offset[None, :] == route_offset[:, None]
    earlier = unit_index[None, :] < unit_index[:, None]
    unit_rank = jnp.sum((same_offset & earlier).astype(jnp.int32), axis=1)
    place = route_offset * slots + unit_rank
    slot_index = jnp.arange(slot_total, dtype=jnp.int32)
    picked = unit_count + jnp.sum(
        jnp.where(place[None, :] == slot_index[:, None], unit_index[None, :] - unit_count, 0),
        axis=1,
    )
    block = (states, states)
    smem = pl.BlockSpec(memory_space=pltpu.SMEM)
    vmem = pl.BlockSpec(memory_space=pltpu.VMEM)
    hbm = pl.BlockSpec(memory_space=pl.ANY)
    return pl.pallas_call(
        functools.partial(kernel, members, slots),
        out_shape=jax.ShapeDtypeStruct(two_site.shape, two_site.dtype),
        in_specs=[smem, smem, smem, smem, vmem, hbm, hbm],
        out_specs=vmem,
        scratch_shapes=[
            pltpu.VMEM((unit_count,) + block, jnp.bfloat16),
            pltpu.VMEM((unit_count,) + block, jnp.bfloat16),
            pltpu.VMEM((slot_total,) + block, jnp.bfloat16),
            pltpu.VMEM((slot_total,) + block, jnp.bfloat16),
            pltpu.VMEM((unit_count,) + block, jnp.bfloat16),
            pltpu.VMEM((sec_local + 2,) + block, jnp.bfloat16),
            pltpu.VMEM((sec_local,) + block, jnp.float32),
            pltpu.SemaphoreType.DMA,
            pltpu.SemaphoreType.DMA,
            pltpu.SemaphoreType.DMA((2,)),
            pltpu.SemaphoreType.DMA((2,)),
            pltpu.SemaphoreType.DMA((members,)),
            pltpu.SemaphoreType.DMA((members,)),
        ],
        compiler_params=pltpu.CompilerParams(
            collective_id=0, has_side_effects=True, vmem_limit_bytes=50 * 1024 * 1024
        ),
        name="route_and_multiply",
    )(
        picked,
        term_shift,
        left_size,
        right_size,
        two_site,
        left_env.reshape((unit_count,) + block),
        right_env,
    )


def solution(mesh):
    in_specs = (
        P(("groups", "sec"), None, None),
        P(("groups", "sec")),
        P(("groups", "sec")),
        P("groups"),
        P("groups"),
        P(("groups", "sec"), None, None, None),
        P(("groups", "sec"), None, None),
    )
    out_specs = P(("groups", "sec"), None, None)
    return jax.shard_map(local, mesh=mesh, in_specs=in_specs, out_specs=out_specs, check_vma=False)
```

```python
import functools

import jax
import jax.numpy as jnp
from jax import lax
from jax.experimental import pallas as pl
from jax.experimental.pallas import tpu as pltpu
from jax.sharding import PartitionSpec as P


def live_region(rows, columns, states):
    row = lax.broadcasted_iota(jnp.int32, (states, states), 0)
    column = lax.broadcasted_iota(jnp.int32, (states, states), 1)
    return (row < rows) & (column < columns)


def kernel(
    members,
    slots,
    numbers,
    two_site_hbm,
    left_env_hbm,
    right_env_hbm,
    out_ref,
    two_site,
    left_env,
    right_env,
    outgoing,
    incoming,
    projected,
    padded,
    total,
    load_sem,
    edge_send_sem,
    edge_recv_sem,
    send_sem,
    recv_sem,
):
    own = lax.axis_index("sec")
    sec_local, states = two_site.shape[0], two_site.shape[1]
    unit_count = left_env.shape[0]
    term_count = unit_count // sec_local
    half = members // 2
    own_half, own_place = own // half, own % half

    shift_start = members * slots
    left_start = shift_start + term_count
    right_start = left_start + sec_local

    two_site_copy = pltpu.make_async_copy(two_site_hbm, two_site, load_sem.at[0])
    right_copy = pltpu.make_async_copy(right_env_hbm, right_env, load_sem.at[1])
    left_copy = pltpu.make_async_copy(left_env_hbm, left_env, load_sem.at[2])
    two_site_copy.start()
    right_copy.start()

    barrier = pltpu.get_barrier_semaphore()

    def greet(step, carry):
        pl.semaphore_signal(barrier, inc=1, device_id={"sec": lax.rem(own + step, members)})
        return carry

    lax.fori_loop(1, members, greet, 0)

    two_site_copy.wait()
    for sector in range(sec_local):
        live = live_region(numbers[left_start + sector], numbers[right_start + sector], states)
        block = two_site[sector]
        padded[1 + sector] = jnp.where(live, block, jnp.zeros_like(block))

    pl.semaphore_wait(barrier, members - 1)

    def edge_copy(source, target, index, peer):
        return pltpu.make_async_remote_copy(
            src_ref=padded.at[source],
            dst_ref=padded.at[target],
            send_sem=edge_send_sem.at[index],
            recv_sem=edge_recv_sem.at[index],
            device_id={"sec": peer},
        )

    up = edge_copy(sec_local, 0, 0, lax.rem(own + 1, members))
    down = edge_copy(1, sec_local + 1, 1, lax.rem(own + members - 1, members))
    has_up, has_down = own < members - 1, own > 0

    pl.when(has_up)(up.start)
    pl.when(has_down)(down.start)

    def partner(step, sign):
        across = step < half
        move = jnp.where(across, step, step - half + 1)
        base = jnp.where(across, 1 - own_half, own_half) * half
        return base + lax.rem(own_place + sign * move + half, half)

    def block_copy(step):
        return pltpu.make_async_remote_copy(
            src_ref=outgoing.at[pl.ds(step * slots, slots)],
            dst_ref=incoming.at[pl.ds(step * slots, slots)],
            send_sem=send_sem.at[step],
            recv_sem=recv_sem.at[step],
            device_id={"sec": partner(step, 1)},
        )

    right_copy.wait()
    left_copy.start()

    def send(step, carry):
        offset = lax.rem(own - partner(step, 1) + members, members)
        for slot in range(slots):
            unit = jnp.minimum(numbers[offset * slots + slot], unit_count - 1)
            outgoing[step * slots + slot] = right_env[unit]
        block_copy(step).start()
        return carry

    lax.fori_loop(0, members - 1, send, 0)
    for slot in range(slots):
        unit = jnp.minimum(numbers[slot], unit_count - 1)
        incoming[(members - 1) * slots + slot] = right_env[unit]

    @pl.when(own == 0)
    def _():
        padded[0] = jnp.zeros(padded.shape[1:], padded.dtype)

    @pl.when(own == members - 1)
    def _():
        padded[sec_local + 1] = jnp.zeros(padded.shape[1:], padded.dtype)

    pl.when(has_up)(up.wait_send)
    pl.when(has_down)(down.wait_send)
    pl.when(has_down)(up.wait_recv)
    pl.when(has_up)(down.wait_recv)
    left_copy.wait()

    def project(unit, carry):
        source = padded[unit // term_count + 1 - numbers[shift_start + unit % term_count]]
        projected[unit] = jnp.dot(
            left_env[unit], source, preferred_element_type=jnp.float32
        ).astype(jnp.bfloat16)
        return carry

    lax.fori_loop(0, unit_count, project, 0)

    total[...] = jnp.zeros_like(total)

    def multiply(step, offset):
        units = [numbers[offset * slots + slot] for slot in range(slots)]
        factors = [projected[jnp.minimum(unit, unit_count - 1)] for unit in units]
        rights = jnp.concatenate([incoming[step * slots + slot] for slot in range(slots)], axis=1)
        for sector in range(sec_local):
            lefts = jnp.concatenate(
                [
                    jnp.where(unit // term_count == sector, factor, jnp.zeros_like(factor))
                    for unit, factor in zip(units, factors)
                ],
                axis=1,
            )
            total[sector] += lax.dot_general(
                lefts, rights, (((1,), (1,)), ((), ())), preferred_element_type=jnp.float32
            )

    multiply(members - 1, 0)

    def arrive(step, carry):
        turn = lax.rem(step + half, members - 1)
        offset = lax.rem(partner(turn, -1) - own + members, members)
        block_copy(turn).wait_recv()
        multiply(turn, offset)
        return carry

    lax.fori_loop(0, members - 1, arrive, 0)

    def sent(step, carry):
        block_copy(step).wait_send()
        return carry

    lax.fori_loop(0, members - 1, sent, 0)

    for sector in range(sec_local):
        live = live_region(numbers[left_start + sector], numbers[right_start + sector], states)
        value = total[sector]
        out_ref[sector] = jnp.where(live, value, jnp.zeros_like(value)).astype(out_ref.dtype)


def local(two_site, left_size, right_size, term_shift, route_offset, left_env, right_env):
    members = lax.axis_size("sec")
    sec_local, states = two_site.shape[0], two_site.shape[1]
    unit_count = right_env.shape[0]
    slots = (unit_count + members - 1) // members
    slot_total = members * slots
    unit_index = jnp.arange(unit_count, dtype=jnp.int32)
    same_offset = route_offset[None, :] == route_offset[:, None]
    earlier = unit_index[None, :] < unit_index[:, None]
    unit_rank = jnp.sum((same_offset & earlier).astype(jnp.int32), axis=1)
    place = route_offset * slots + unit_rank
    slot_index = jnp.arange(slot_total, dtype=jnp.int32)
    picked = unit_count + jnp.sum(
        jnp.where(place[None, :] == slot_index[:, None], unit_index[None, :] - unit_count, 0),
        axis=1,
    )
    numbers = jnp.concatenate([picked, term_shift, left_size, right_size])
    block = (states, states)
    hbm = pl.BlockSpec(memory_space=pl.ANY)
    return pl.pallas_call(
        functools.partial(kernel, members, slots),
        out_shape=jax.ShapeDtypeStruct(two_site.shape, two_site.dtype),
        in_specs=[pl.BlockSpec(memory_space=pltpu.SMEM), hbm, hbm, hbm],
        out_specs=pl.BlockSpec(memory_space=pltpu.VMEM),
        scratch_shapes=[
            pltpu.VMEM(two_site.shape, jnp.bfloat16),
            pltpu.VMEM((unit_count,) + block, jnp.bfloat16),
            pltpu.VMEM((unit_count,) + block, jnp.bfloat16),
            pltpu.VMEM((slot_total,) + block, jnp.bfloat16),
            pltpu.VMEM((slot_total,) + block, jnp.bfloat16),
            pltpu.VMEM((unit_count,) + block, jnp.bfloat16),
            pltpu.VMEM((sec_local + 2,) + block, jnp.bfloat16),
            pltpu.VMEM((sec_local,) + block, jnp.float32),
            pltpu.SemaphoreType.DMA((3,)),
            pltpu.SemaphoreType.DMA((2,)),
            pltpu.SemaphoreType.DMA((2,)),
            pltpu.SemaphoreType.DMA((members - 1,)),
            pltpu.SemaphoreType.DMA((members - 1,)),
        ],
        compiler_params=pltpu.CompilerParams(
            collective_id=0, has_side_effects=True, vmem_limit_bytes=50 * 1024 * 1024
        ),
        name="route_and_multiply",
    )(numbers, two_site, left_env.reshape((unit_count,) + block), right_env)


def solution(mesh):
    in_specs = (
        P(("groups", "sec"), None, None),
        P(("groups", "sec")),
        P(("groups", "sec")),
        P("groups"),
        P("groups"),
        P(("groups", "sec"), None, None, None),
        P(("groups", "sec"), None, None),
    )
    out_specs = P(("groups", "sec"), None, None)
    return jax.shard_map(local, mesh=mesh, in_specs=in_specs, out_specs=out_specs, check_vma=False)
```

```python
import functools

import jax
import jax.numpy as jnp
from jax import lax
from jax.experimental import pallas as pl
from jax.experimental.pallas import tpu as pltpu
from jax.sharding import PartitionSpec as P


def live_region(rows, columns, states):
    row = lax.broadcasted_iota(jnp.int32, (states, states), 0)
    column = lax.broadcasted_iota(jnp.int32, (states, states), 1)
    return (row < rows) & (column < columns)


def kernel(
    members,
    slots,
    numbers,
    two_site_hbm,
    left_env_hbm,
    right_env_hbm,
    out_ref,
    two_site,
    left_env,
    right_env,
    outgoing,
    incoming,
    projected,
    padded,
    total,
    load_sem,
    edge_send_sem,
    edge_recv_sem,
    send_sem,
    recv_sem,
):
    own = lax.axis_index("sec")
    sec_local, states = two_site.shape[0], two_site.shape[1]
    unit_count = left_env.shape[0]
    term_count = unit_count // sec_local
    quarter = members // 4
    own_quarter, own_place = own // quarter, own % quarter

    shift_start = members * slots
    left_start = shift_start + term_count
    right_start = left_start + sec_local

    two_site_copy = pltpu.make_async_copy(two_site_hbm, two_site, load_sem.at[0])
    right_copy = pltpu.make_async_copy(right_env_hbm, right_env, load_sem.at[1])
    left_copy = pltpu.make_async_copy(left_env_hbm, left_env, load_sem.at[2])
    two_site_copy.start()
    right_copy.start()

    barrier = pltpu.get_barrier_semaphore()

    def greet(step, carry):
        pl.semaphore_signal(barrier, inc=1, device_id={"sec": lax.rem(own + step, members)})
        return carry

    lax.fori_loop(1, members, greet, 0)

    two_site_copy.wait()
    for sector in range(sec_local):
        live = live_region(numbers[left_start + sector], numbers[right_start + sector], states)
        block = two_site[sector]
        padded[1 + sector] = jnp.where(live, block, jnp.zeros_like(block))

    pl.semaphore_wait(barrier, members - 1)

    def edge_copy(source, target, index, peer):
        return pltpu.make_async_remote_copy(
            src_ref=padded.at[source],
            dst_ref=padded.at[target],
            send_sem=edge_send_sem.at[index],
            recv_sem=edge_recv_sem.at[index],
            device_id={"sec": peer},
        )

    up = edge_copy(sec_local, 0, 0, lax.rem(own + 1, members))
    down = edge_copy(1, sec_local + 1, 1, lax.rem(own + members - 1, members))
    has_up, has_down = own < members - 1, own > 0

    pl.when(has_up)(up.start)
    pl.when(has_down)(down.start)

    def partner(step, sign):
        group = step // quarter
        move = jnp.where(group < 3, step % quarter, step - 3 * quarter + 1)
        ahead, back = (2 * own_quarter + 1) % 5, (3 * own_quarter + 2) % 5
        if sign < 0:
            ahead, back = back, ahead
        other = jnp.where(
            group == 0,
            ahead,
            jnp.where(group == 1, 3 - own_quarter, jnp.where(group == 2, back, own_quarter)),
        )
        return other * quarter + lax.rem(own_place + sign * move + quarter, quarter)

    def block_copy(step):
        return pltpu.make_async_remote_copy(
            src_ref=outgoing.at[pl.ds(step * slots, slots)],
            dst_ref=incoming.at[pl.ds(step * slots, slots)],
            send_sem=send_sem.at[step],
            recv_sem=recv_sem.at[step],
            device_id={"sec": partner(step, 1)},
        )

    right_copy.wait()
    left_copy.start()

    def send(step, carry):
        offset = lax.rem(own - partner(step, 1) + members, members)
        for slot in range(slots):
            unit = jnp.minimum(numbers[offset * slots + slot], unit_count - 1)
            outgoing[step * slots + slot] = right_env[unit]
        block_copy(step).start()
        return carry

    lax.fori_loop(0, members - 1, send, 0)
    for slot in range(slots):
        unit = jnp.minimum(numbers[slot], unit_count - 1)
        incoming[(members - 1) * slots + slot] = right_env[unit]

    @pl.when(own == 0)
    def _():
        padded[0] = jnp.zeros(padded.shape[1:], padded.dtype)

    @pl.when(own == members - 1)
    def _():
        padded[sec_local + 1] = jnp.zeros(padded.shape[1:], padded.dtype)

    pl.when(has_up)(up.wait_send)
    pl.when(has_down)(down.wait_send)
    pl.when(has_down)(up.wait_recv)
    pl.when(has_up)(down.wait_recv)
    left_copy.wait()

    def project(unit, carry):
        source = padded[unit // term_count + 1 - numbers[shift_start + unit % term_count]]
        projected[unit] = jnp.dot(
            left_env[unit], source, preferred_element_type=jnp.float32
        ).astype(jnp.bfloat16)
        return carry

    lax.fori_loop(0, unit_count, project, 0)

    total[...] = jnp.zeros_like(total)

    def multiply(step, offset):
        units = [numbers[offset * slots + slot] for slot in range(slots)]
        factors = [projected[jnp.minimum(unit, unit_count - 1)] for unit in units]
        rights = jnp.concatenate([incoming[step * slots + slot] for slot in range(slots)], axis=1)
        for sector in range(sec_local):
            lefts = jnp.concatenate(
                [
                    jnp.where(unit // term_count == sector, factor, jnp.zeros_like(factor))
                    for unit, factor in zip(units, factors)
                ],
                axis=1,
            )
            total[sector] += lax.dot_general(
                lefts, rights, (((1,), (1,)), ((), ())), preferred_element_type=jnp.float32
            )

    multiply(members - 1, 0)

    def arrive(step, carry):
        turn = lax.rem(step + 3 * quarter, members - 1)
        offset = lax.rem(partner(turn, -1) - own + members, members)
        block_copy(turn).wait_recv()
        multiply(turn, offset)
        return carry

    lax.fori_loop(0, members - 1, arrive, 0)

    def sent(step, carry):
        block_copy(step).wait_send()
        return carry

    lax.fori_loop(0, members - 1, sent, 0)

    for sector in range(sec_local):
        live = live_region(numbers[left_start + sector], numbers[right_start + sector], states)
        value = total[sector]
        out_ref[sector] = jnp.where(live, value, jnp.zeros_like(value)).astype(out_ref.dtype)


def local(two_site, left_size, right_size, term_shift, route_offset, left_env, right_env):
    members = lax.axis_size("sec")
    sec_local, states = two_site.shape[0], two_site.shape[1]
    unit_count = right_env.shape[0]
    slots = (unit_count + members - 1) // members
    slot_total = members * slots
    unit_index = jnp.arange(unit_count, dtype=jnp.int32)
    same_offset = route_offset[None, :] == route_offset[:, None]
    earlier = unit_index[None, :] < unit_index[:, None]
    unit_rank = jnp.sum((same_offset & earlier).astype(jnp.int32), axis=1)
    place = route_offset * slots + unit_rank
    slot_index = jnp.arange(slot_total, dtype=jnp.int32)
    picked = unit_count + jnp.sum(
        jnp.where(place[None, :] == slot_index[:, None], unit_index[None, :] - unit_count, 0),
        axis=1,
    )
    numbers = jnp.concatenate([picked, term_shift, left_size, right_size])
    block = (states, states)
    hbm = pl.BlockSpec(memory_space=pl.ANY)
    return pl.pallas_call(
        functools.partial(kernel, members, slots),
        out_shape=jax.ShapeDtypeStruct(two_site.shape, two_site.dtype),
        in_specs=[pl.BlockSpec(memory_space=pltpu.SMEM), hbm, hbm, hbm],
        out_specs=pl.BlockSpec(memory_space=pltpu.VMEM),
        scratch_shapes=[
            pltpu.VMEM(two_site.shape, jnp.bfloat16),
            pltpu.VMEM((unit_count,) + block, jnp.bfloat16),
            pltpu.VMEM((unit_count,) + block, jnp.bfloat16),
            pltpu.VMEM((slot_total,) + block, jnp.bfloat16),
            pltpu.VMEM((slot_total,) + block, jnp.bfloat16),
            pltpu.VMEM((unit_count,) + block, jnp.bfloat16),
            pltpu.VMEM((sec_local + 2,) + block, jnp.bfloat16),
            pltpu.VMEM((sec_local,) + block, jnp.float32),
            pltpu.SemaphoreType.DMA((3,)),
            pltpu.SemaphoreType.DMA((2,)),
            pltpu.SemaphoreType.DMA((2,)),
            pltpu.SemaphoreType.DMA((members - 1,)),
            pltpu.SemaphoreType.DMA((members - 1,)),
        ],
        compiler_params=pltpu.CompilerParams(
            collective_id=0, has_side_effects=True, vmem_limit_bytes=50 * 1024 * 1024
        ),
        name="route_and_multiply",
    )(numbers, two_site, left_env.reshape((unit_count,) + block), right_env)


def solution(mesh):
    in_specs = (
        P(("groups", "sec"), None, None),
        P(("groups", "sec")),
        P(("groups", "sec")),
        P("groups"),
        P("groups"),
        P(("groups", "sec"), None, None, None),
        P(("groups", "sec"), None, None),
    )
    out_specs = P(("groups", "sec"), None, None)
    return jax.shard_map(local, mesh=mesh, in_specs=in_specs, out_specs=out_specs, check_vma=False)
```
